32 devices in a mesh: grp: 2 (over x), head: 8 (over z, y), tok: 2 (over core).
Axes of the slice: x: 2, y: 2, z: 4, core: 2. Of those that a mesh axis runs over, the one named last changes fastest.
Arguments:
- queries: bfloat16 [1024, 16384], P(('grp', 'tok'), 'head'), parts along dimension 0, may hold values from -18 to 18
- key_rows: bfloat16 [1024, 1024], P(('grp', 'tok')), parts along dimension 0, may hold values from -5 to 5
- values: bfloat16 [1024, 1024], P(('grp', 'tok')), parts along dimension 0, may hold values from -15 to 15
- sign_bits: int32 [16384], replicated, may hold values from 0 to 1
Outputs:
- hessian: bfloat16 [32768, 16384], P(('grp', 'tok'), 'head'), parts along dimension 0
The draws below stay inside these ranges and needn't reach their ends.
There are 2 independent parts, one for each index of `grp`. The reference program is written for one: setup_inputs(seed, part) draws one part's arguments, and reference() takes and returns one part's arrays. A program takes and returns all parts, laid end to end along the dimension named above; an argument that names none is the same for every part. Nothing has to cross between parts.
All inputs are finite; a program needn't handle non-finite values.
Results may differ from the reference program's by a relative error of at most 0.0055.
Values may be sent and summed in bfloat16 or wider, within the bound.
No kernel may reach another device: no remote copies, remote signals or barrier semaphores. Data moves between devices by JAX's collectives and lax.ppermute only.
A program may use at most 448 MiB of HBM per device.

```python
import math
import jax
import jax.numpy as jnp
from jax import lax

HEADS = 128
KV_HEADS = 8
DH = 128
D = 16384
KVD = 1024
GROUP = 16
TOKENS = 512


def draw_queries(key, part):
    key = jax.random.fold_in(key, 11)
    drawn = jnp.clip(jax.random.normal(key, (TOKENS, D), jnp.float32), -5.0, 5.0)
    return drawn.astype(jnp.bfloat16)


def draw_key_rows(key, part):
    key = jax.random.fold_in(key, 23)
    drawn = jnp.clip(jax.random.normal(key, (TOKENS, KVD), jnp.float32), -5.0, 5.0)
    return drawn.astype(jnp.bfloat16)


def set_ends(drawn, own_key, least, largest):
    longest = drawn.shape.index(max(drawn.shape))
    spots = []
    for shift in (0, 1):
        where = [jax.random.randint(jax.random.fold_in(own_key, axis), (), 0, length) for axis, length in enumerate(drawn.shape)]
        where[longest] = (where[longest] + shift) % drawn.shape[longest]
        spots.append(tuple(where))
    return drawn.at[spots[0]].set(least).at[spots[1]].set(largest)


def steps_of(own_key, shape, pieces, low, largest):
    loudness, own = 1.0, jax.random.fold_in(own_key, 6)
    for dim, parts in pieces:
        steps = jnp.exp(jax.random.uniform(jax.random.fold_in(own, dim), (parts,), jnp.float32, low / len(pieces), largest / len(pieces)))
        loudness = loudness * jnp.repeat(steps, shape[dim] // parts).reshape([-1 if axis == dim else 1 for axis in range(len(shape))])
    return loudness


def centred(key, extent, spread, bound, split=(), kind=jnp.bfloat16):
    drawn = spread * jax.random.normal(key, extent, jnp.float32)
    if split:
        drawn = drawn * steps_of(key, extent, split, -0.22, 0.18)
    return jnp.clip(drawn, -bound, bound).astype(kind)


def setup_inputs(seed: int = 0, part: int = 0) -> dict:
    seeds = jax.random.split(jax.random.key(seed), 5)
    own_keys = jax.random.split(jax.random.fold_in(seeds[4], part), 5)
    return {
        "queries": draw_queries(jax.random.fold_in(jax.random.fold_in(seeds[4], part), 71), part),
        "key_rows": draw_key_rows(jax.random.fold_in(jax.random.fold_in(seeds[4], part), 71), part),
        "values": centred(own_keys[2], (TOKENS, KVD), 3.0, 15.0, ((0, 2),)),
        "sign_bits": set_ends(jax.random.randint(seeds[3], (D,), 0, 2), jax.random.fold_in(seeds[3], 1), 0, 1).astype(jnp.int32),
    }


def sylvester(order):
    counter = jnp.arange(order, dtype=jnp.int32)
    anded = counter[:, None] & counter[None, :]
    parity = jnp.zeros_like(anded)
    for bit_level in range(max(order.bit_length(), 1)):
        parity = parity ^ anded >> bit_level & 1
    return (1 - 2 * parity).astype(jnp.float32)

def reference(queries, key_rows, values, sign_bits):
    query_heads = queries.reshape(TOKENS, HEADS, DH).astype(jnp.float32)
    key_heads = jnp.repeat(key_rows.reshape(TOKENS, KV_HEADS, DH), GROUP, axis=1).astype(jnp.float32)
    value_heads = jnp.repeat(values.reshape(TOKENS, KV_HEADS, DH), GROUP, axis=1).astype(jnp.float32)
    scores = jnp.einsum('thd,shd->hts', query_heads, key_heads) * (1.0 / math.sqrt(DH))
    row_pos = jnp.arange(TOKENS, dtype=jnp.int32)[:, None]
    col_pos = jnp.arange(TOKENS, dtype=jnp.int32)[None, :]
    causal_mask = col_pos <= row_pos
    scores = jnp.where(causal_mask[None], scores, -1e+30)
    row_max = lax.optimization_barrier(jnp.max(scores, axis=-1, keepdims=True))
    expo = jnp.exp(scores - row_max)
    row_total = lax.optimization_barrier(jnp.sum(expo, axis=-1, keepdims=True))
    weights = expo.astype(jnp.bfloat16).astype(jnp.float32)
    attended = jnp.einsum('hts,shd->htd', weights, value_heads) / row_total
    sign_vals = (1 - 2 * sign_bits).astype(jnp.float32).reshape(HEADS, 1, DH)
    inner_rot = jnp.einsum('htd,de->the', attended * sign_vals, sylvester(DH), precision=lax.Precision.HIGHEST)
    inner_rot = (inner_rot * (1.0 / math.sqrt(DH))).astype(jnp.bfloat16)
    mixed = jnp.einsum('rhe,hg->rge', inner_rot.astype(jnp.float32), sylvester(HEADS)) * (1.0 / math.sqrt(HEADS))
    rotated = mixed.astype(jnp.bfloat16).reshape(TOKENS, D)
    block = 512
    blocks = rotated.reshape(TOKENS, D // block, block).transpose(1, 0, 2)

    def strip_gram(column_block):
        gram = jnp.dot(rotated.T, column_block, preferred_element_type=jnp.float32)
        return (gram * (2.0 / TOKENS)).astype(jnp.bfloat16)
    strips = lax.map(strip_gram, blocks)
    return strips.transpose(1, 0, 2).reshape(D, D)
```

```python
import functools
import math

import jax
import jax.numpy as jnp
from jax import lax
from jax.experimental import pallas as pl
from jax.experimental.pallas import tpu as pltpu
from jax.sharding import PartitionSpec as P

HEADS = 128
DH = 128
MIB = 1024 * 1024
ATTEND_UNROLL = 4
MIX_WAIT, MIX_DUE = 1, 4
GRAM_WAIT, GRAM_DUE = 3, 6


def butterfly(tiles):
    if len(tiles) == 1:
        return tiles
    half = len(tiles) // 2
    low = [tiles[i] + tiles[i + half] for i in range(half)]
    high = [tiles[i] - tiles[i + half] for i in range(half)]
    return butterfly(low) + butterfly(high)


def nt_dot(left, right):
    return lax.dot_general(left, right, (((1,), (1,)), ((), ())), preferred_element_type=jnp.float32)


def ring_place(device, devices):
    if devices != 8:
        return device
    upward = device // 2
    return jnp.where(lax.rem(device, 2) == 0, upward, devices - 1 - upward)


def ring_device(place, devices):
    if devices != 8:
        return place
    return jnp.where(place < devices // 2, 2 * place, 2 * (devices - 1 - place) + 1)


def attend_kernel(kv_share, unroll, q_hbm, ko_hbm, vo_hbm, sign_hbm, kp_any, vp_any, out_ref, *scratch):
    q_ref, kv_ref, sign_ref, inner_ref, vt_ref, bar_ref, sem = scratch
    rows, width = q_ref.shape
    heads = width // DH
    scale = math.log2(math.e) / math.sqrt(DH)
    first_head = lax.axis_index("head") * heads
    columns = pl.ds(pl.multiple_of(first_head // kv_share * DH, DH), DH)
    copies = [
        pltpu.make_async_copy(ko_hbm.at[:, columns], kv_ref.at[0], sem.at[0]),
        pltpu.make_async_copy(kp_any.at[:, columns], kv_ref.at[1], sem.at[1]),
        pltpu.make_async_copy(vo_hbm.at[:, columns], kv_ref.at[2], sem.at[2]),
        pltpu.make_async_copy(vp_any.at[:, columns], kv_ref.at[3], sem.at[3]),
        pltpu.make_async_copy(sign_hbm, sign_ref, sem.at[4]),
        pltpu.make_async_copy(q_hbm, q_ref, sem.at[5]),
    ]
    for copy in copies:
        copy.start()
    core = lax.axis_index("tok")
    key_pos = lax.broadcasted_iota(jnp.int32, (rows, rows), 0)
    query_pos = lax.broadcasted_iota(jnp.int32, (rows, rows), 1)
    bar_ref[...] = jnp.where(key_pos <= query_pos, 0.0, -1e30)
    anded = lax.broadcasted_iota(jnp.int32, (DH, DH), 0) & lax.broadcasted_iota(jnp.int32, (DH, DH), 1)
    odd = jnp.zeros_like(anded)
    for level in range(7):
        odd = odd ^ (anded >> level) & 1
    table = (1 - 2 * odd).astype(jnp.float32)
    for copy in copies[2:4]:
        copy.wait()
    vt_ref[:, :rows] = kv_ref[3].astype(jnp.float32).T.astype(jnp.bfloat16)
    vt_ref[:, rows:] = kv_ref[2].astype(jnp.float32).T.astype(jnp.bfloat16)
    for copy in copies[:2] + copies[4:]:
        copy.wait()

    def one(h, earlier):
        q = q_ref[:, pl.ds(pl.multiple_of(h * DH, DH), DH)]
        own = nt_dot(kv_ref[0], q) + bar_ref[...]
        top = jnp.max(own, axis=0, keepdims=True)
        if earlier:
            before = nt_dot(kv_ref[1], q)
            top = jnp.maximum(top, jnp.max(before, axis=0, keepdims=True))
        weights = jnp.exp2((own - top) * scale)
        total = jnp.sum(weights, axis=0, keepdims=True)
        attended = jnp.dot(vt_ref[:, rows:], weights.astype(jnp.bfloat16), preferred_element_type=jnp.float32)
        if earlier:
            weights = jnp.exp2((before - top) * scale)
            total += jnp.sum(weights, axis=0, keepdims=True)
            attended += jnp.dot(vt_ref[:, :rows], weights.astype(jnp.bfloat16), preferred_element_type=jnp.float32)
        attended = attended * (1.0 / total)
        coarse = attended.astype(jnp.bfloat16)
        fine = (attended - coarse.astype(jnp.float32)).astype(jnp.bfloat16)
        signs = (1 - 2 * sign_ref[pl.ds(first_head + h, 1), :]).astype(jnp.float32)
        turn = (table * signs).astype(jnp.bfloat16)
        inner = jnp.dot(turn, coarse, preferred_element_type=jnp.float32) + jnp.dot(
            turn, fine, preferred_element_type=jnp.float32
        )
        inner_ref[h] = (inner * (1.0 / math.sqrt(DH))).astype(jnp.bfloat16)

    unroll = math.gcd(heads, unroll)

    def every(earlier):
        @pl.loop(0, heads // unroll)
        def _(step):
            for u in range(unroll):
                one(step * unroll + u, earlier)

    pl.when(core > 0)(lambda: every(True))
    pl.when(core == 0)(lambda: every(False))

    shrink = 1.0 / math.sqrt(heads)

    @pl.loop(0, DH // 16)
    def _(block):
        band = pl.ds(pl.multiple_of(block * 16, 16), 16)
        for lane in range(0, rows, 128):
            tiles = [inner_ref[h, band, lane : lane + 128].astype(jnp.float32) for h in range(heads)]
            for h, tile in enumerate(butterfly(tiles)):
                at = pl.ds(pl.multiple_of(h * DH + block * 16, 16), 16)
                out_ref[at, lane : lane + 128] = (tile * shrink).astype(jnp.bfloat16)


def attend(queries, own_keys, own_values, signs, prev_keys, prev_values):
    rows, width = queries.shape
    kv_share = HEADS // (own_keys.shape[1] // DH)
    heads = width // DH
    hbm, anywhere = pl.BlockSpec(memory_space=pltpu.HBM), pl.BlockSpec(memory_space=pl.ANY)
    return pl.pallas_call(
        functools.partial(attend_kernel, kv_share, ATTEND_UNROLL),
        in_specs=[hbm] * 4 + [anywhere] * 2,
        out_specs=pl.BlockSpec(memory_space=pltpu.VMEM),
        scratch_shapes=[
            pltpu.VMEM((rows, width), jnp.bfloat16),
            pltpu.VMEM((4, rows, DH), jnp.bfloat16),
            pltpu.VMEM((HEADS, DH), jnp.int32),
            pltpu.VMEM((heads, DH, rows), jnp.bfloat16),
            pltpu.VMEM((DH, 2 * rows), jnp.bfloat16),
            pltpu.VMEM((rows, rows), jnp.float32),
            pltpu.SemaphoreType.DMA((6,)),
        ],
        out_shape=jax.ShapeDtypeStruct((width, rows), jnp.bfloat16),
        compiler_params=pltpu.CompilerParams(vmem_limit_bytes=60 * MIB),
        cost_estimate=pl.CostEstimate(flops=20000000000, bytes_accessed=1024, transcendentals=0),
        name="attend",
    )(queries, own_keys, own_values, signs, prev_keys, prev_values)


def mix_kernel(devices, offset, *refs):
    count = devices + 1
    pieces, (keep_ref, send_ref, held, sem) = refs[:count], refs[count:]
    rows = keep_ref.shape[1]
    lanes = keep_ref.shape[2]
    half = devices // 2
    head, core = lax.axis_index("head"), lax.axis_index("tok")
    place = ring_place(head, devices)
    shifts = [0] + [shift for step in range(1, half) for shift in (devices - step, step)] + [half]
    slots = [ring_device(lax.rem(place + shift, devices), devices) for shift in shifts]
    copies = []
    for p, piece in enumerate(pieces):
        if p == 0:
            source, target = piece.at[pl.ds(offset, rows), :], held.at[slots[0]]
        elif p < devices - 1:
            source, target = piece, held.at[slots[p]]
        else:
            part = (p - (devices - 1)) * (rows // 2)
            source, target = piece, held.at[slots[devices - 1], pl.ds(part, rows // 2), :]
        copies.append(pltpu.make_async_copy(source, target, sem.at[p]))
    for copy in copies:
        copy.start()
    for copy in copies:
        copy.wait()
    flip = jnp.where(core > 0, -1.0, 1.0).astype(jnp.float32)
    shrink = 1.0 / math.sqrt(devices)
    in_keep = (head // half) == core
    own_slot = lax.rem(head, half)

    @pl.loop(0, rows // 16)
    def _(block):
        band = pl.ds(pl.multiple_of(block * 16, 16), 16)
        for lane in range(0, lanes, 128):
            span = slice(lane, lane + 128)
            tiles = [held[d, band, span].astype(jnp.float32) for d in range(devices)]
            flipped = [tiles[d + half] * flip for d in range(half)]
            stay = butterfly([tiles[d] + flipped[d] for d in range(half)])
            leave = butterfly([tiles[d] - flipped[d] for d in range(half)])
            for d in range(half):
                keep_ref[d, band, span] = (stay[d] * shrink).astype(jnp.bfloat16)
                send_ref[d, band, span] = (leave[d] * shrink).astype(jnp.bfloat16)

    @pl.when(in_keep)
    def _():
        strip = keep_ref[own_slot]
        keep_ref[half] = strip
        send_ref[half] = strip

    @pl.when(jnp.logical_not(in_keep))
    def _():
        strip = send_ref[own_slot]
        keep_ref[half] = strip
        send_ref[half] = strip


def mix(devices, offset, rows, own, pieces):
    lanes = own.shape[1]
    half = devices // 2
    shape = (half + 1, rows, lanes)
    return pl.pallas_call(
        functools.partial(mix_kernel, devices, offset),
        in_specs=[pl.BlockSpec(memory_space=pl.ANY)] * (devices + 1),
        out_specs=[pl.BlockSpec(memory_space=pltpu.VMEM)] * 2,
        scratch_shapes=[
            pltpu.VMEM((devices, rows, lanes), jnp.bfloat16),
            pltpu.SemaphoreType.DMA((devices + 1,)),
        ],
        out_shape=[jax.ShapeDtypeStruct(shape, jnp.bfloat16)] * 2,
        compiler_params=pltpu.CompilerParams(vmem_limit_bytes=24 * MIB),
        cost_estimate=pl.CostEstimate(flops=20000000000, bytes_accessed=1024, transcendentals=0),
        name="mix",
    )(own, *pieces)


def gram_kernel(starts, sizes, chunk, scale, aliased, *refs):
    refs = list(refs)
    take = lambda n: [refs.pop(0) for _ in range(n)]
    if aliased:
        take(1)
    keep_rows, recv_rows = take(chunk + 1), take(chunk + 1)
    keep_cols, recv_cols = take(chunk + 1), take(chunk + 1)
    (out_ref,) = take(1)
    wide, sem = take(2)
    tall = take(1)[0] if chunk else None
    r, steps = pl.program_id(0), pl.num_programs(0)
    slot = lax.rem(r, 2)
    first, size = starts[chunk], sizes[chunk]

    def wide_copy(at, s):
        return pltpu.make_async_copy(
            wide.at[s], out_ref.at[at, pl.ds(first, size), pl.ds(0, first + size)], sem.at[0, s]
        )

    def tall_copy(at, s):
        return pltpu.make_async_copy(
            tall.at[s], out_ref.at[at, pl.ds(0, first), pl.ds(first, size)], sem.at[1, s]
        )

    @pl.when(r >= 2)
    def _():
        wide_copy(r - 2, slot).wait()
        if chunk:
            tall_copy(r - 2, slot).wait()

    def block(a_keep, a_recv, b_keep, b_recv, store):
        height, width = a_keep.shape[1], b_keep.shape[1]
        tile_m = math.gcd(height, 256)
        tile_n = math.gcd(width, 512)
        for i in range(0, height, tile_m):
            left, left_other = a_keep[0, i : i + tile_m, :], a_recv[0, i : i + tile_m, :]
            for k in range(0, width, tile_n):
                total = nt_dot(left, b_keep[0, k : k + tile_n, :]) + nt_dot(left_other, b_recv[0, k : k + tile_n, :])
                store(i, tile_m, k, tile_n, (total * scale).astype(jnp.bfloat16))

    for c in range(chunk + 1):

        def store_wide(i, m, k, n, value):
            wide[slot, i : i + m, starts[c] + k : starts[c] + k + n] = value

        block(keep_rows[chunk], recv_rows[chunk], keep_cols[c], recv_cols[c], store_wide)
    wide_copy(r, slot).start()
    for c in range(chunk):

        def store_tall(i, m, k, n, value):
            tall[slot, starts[c] + i : starts[c] + i + m, k : k + n] = value

        block(keep_rows[c], recv_rows[c], keep_cols[chunk], recv_cols[chunk], store_tall)
    if chunk:
        tall_copy(r, slot).start()

    @pl.when(r == steps - 1)
    def _():
        for back in (1, 0):
            at = r - back
            wide_copy(at, lax.rem(at, 2)).wait()
            if chunk:
                tall_copy(at, lax.rem(at, 2)).wait()


def gram(out, keeps, recvs, starts, sizes, chunk, scale, shape):
    half = keeps[0].shape[0] - 1
    lanes = keeps[0].shape[2]
    first, size = starts[chunk], sizes[chunk]
    row_spec = [pl.BlockSpec((1, sizes[c], lanes), lambda r: (r, 0, 0)) for c in range(chunk + 1)]
    col_spec = [pl.BlockSpec((1, sizes[c], lanes), lambda r: (half, 0, 0)) for c in range(chunk + 1)]
    aliased = out is not None
    anywhere = pl.BlockSpec(memory_space=pl.ANY)
    scratch = [pltpu.VMEM((2, size, first + size), jnp.bfloat16), pltpu.SemaphoreType.DMA((2, 2))]
    if chunk:
        scratch.append(pltpu.VMEM((2, first, size), jnp.bfloat16))
    area = half * (size * (first + size) + first * size)
    return pl.pallas_call(
        functools.partial(gram_kernel, starts, sizes, chunk, scale, aliased),
        grid=(half,),
        in_specs=([anywhere] if aliased else []) + row_spec * 2 + col_spec * 2,
        out_specs=anywhere,
        out_shape=jax.ShapeDtypeStruct(shape, jnp.bfloat16),
        scratch_shapes=scratch,
        input_output_aliases={0: 0} if aliased else {},
        compiler_params=pltpu.CompilerParams(vmem_limit_bytes=40 * MIB),
        cost_estimate=pl.CostEstimate(flops=20000000000, bytes_accessed=1024, transcendentals=0),
        name=f"gram{chunk}",
    )(*(([out] if aliased else []) + keeps + recvs + keeps + recvs))


PLANS = {(16, 4): ([4, 4, 4, 4], [0, 1, 0, 1, 0, 1, 0, 2, 1, 2, 3, 2, 3, 2, 3, 3])}


def plan(local_heads, hops):
    if (local_heads, hops) in PLANS:
        return PLANS[local_heads, hops]
    done = [0] * local_heads
    sequence = []
    while min(done) < hops:
        last = sequence[-1] if sequence else -1
        ready = [c for c in range(local_heads) if done[c] < hops]
        pick = next((c for c in ready if c != last), ready[0])
        done[pick] += 1
        sequence.append(pick)
    return [1] * local_heads, sequence


def after(values, *others):
    return lax.optimization_barrier((tuple(values), others))[0]


def local(devices, queries, key_rows, values, sign_bits):
    rows, width = queries.shape
    tok_count = lax.axis_size("tok")
    half = devices // 2
    order = list(range(devices))
    if devices == 8:
        order = order[0::2] + order[:0:-2]
    forward = [(order[i], order[(i + 1) % devices]) for i in range(devices)]
    backward = [(b, a) for a, b in forward]
    prev_keys, prev_values = lax.ppermute((key_rows, values), "tok", [(0, 1)])
    mixed = attend(queries, key_rows, values, sign_bits.reshape(HEADS, DH), prev_keys, prev_values)

    heads_of, sequence = plan(width // DH, half)
    sizes = [c * DH for c in heads_of]
    chunks = len(sizes)
    starts = [sum(sizes[:c]) for c in range(chunks)]
    held = [[mixed[starts[c] : starts[c] + sizes[c]]] * 2 for c in range(chunks)]
    pieces = [[] for _ in range(chunks)]
    scale = 2.0 / (rows * tok_count)
    keeps, recvs, out = [None] * chunks, [None] * chunks, None
    landed, due, pending = [], {}, []
    for k, c in enumerate(sequence):
        going, coming = held[c]
        if len(pieces[c]) == 2 * (half - 1):
            going, coming = going[: sizes[c] // 2], coming[sizes[c] // 2 :]
        waits = landed[max(0, k - 3) : max(0, k - 1)] + due.pop(k, [])
        if waits:
            going, coming = after((going, coming), *waits)
        with jax.named_scope(f"up{k}c{c}"):
            going = lax.ppermute(going, "head", forward)
        with jax.named_scope(f"down{k}c{c}"):
            coming = lax.ppermute(coming, "head", backward)
        landed.append((going, coming))
        held[c] = [going, coming]
        pieces[c] += [going, coming]
        if len(pieces[c]) == 2 * half:
            pending.append(("mix", c, k + MIX_WAIT, k + MIX_DUE))
            pending.append(("gram", c, k + GRAM_WAIT, k + GRAM_DUE))
        final = k == len(sequence) - 1
        for task in list(pending):
            kind, which, ready, deadline = task
            if ready > k and not final:
                continue
            pending.remove(task)
            if kind == "mix":
                own = mixed
                if not final:
                    own, pieces[which] = after((mixed, pieces[which]), landed[k])
                keeps[which], send = mix(devices, starts[which], sizes[which], own, pieces[which])
                with jax.named_scope(f"swap{which}"):
                    recvs[which] = lax.ppermute(send, "tok", [(0, 1), (1, 0)])
                done = keeps[which]
            else:
                n = which + 1
                if not final:
                    keeps[which] = after((keeps[which],), landed[k])[0]
                out = gram(out, keeps[:n], recvs[:n], starts, sizes, which, scale, (half, width, width))
                done = out
            due.setdefault(deadline, []).append(done)
    return out.reshape(half * width, width)


def solution(mesh):
    placed = (P(("grp", "tok"), "head"), P(("grp", "tok"), None), P(("grp", "tok"), None), P())
    return jax.shard_map(
        functools.partial(local, mesh.shape["head"]),
        mesh=mesh,
        in_specs=placed,
        out_specs=P(("grp", "tok"), "head"),
        check_vma=False,
    )
```

```python
import functools
import math

import jax
import jax.numpy as jnp
from jax import lax
from jax.experimental import pallas as pl
from jax.experimental.pallas import tpu as pltpu
from jax.sharding import PartitionSpec as P

HEADS = 128
DH = 128
MIB = 1024 * 1024
ATTEND_UNROLL = 8
DEPTH = 3
GATES = {"mix": (1, 4), "swap": (2, 5), "gram": (3, 6)}


def butterfly(tiles):
    if len(tiles) == 1:
        return tiles
    half = len(tiles) // 2
    low = [tiles[i] + tiles[i + half] for i in range(half)]
    high = [tiles[i] - tiles[i + half] for i in range(half)]
    return butterfly(low) + butterfly(high)


def nt_dot(left, right):
    return lax.dot_general(left, right, (((1,), (1,)), ((), ())), preferred_element_type=jnp.float32)


def ring_place(device, devices):
    if devices != 8:
        return device
    upward = device // 2
    return jnp.where(lax.rem(device, 2) == 0, upward, devices - 1 - upward)


def ring_device(place, devices):
    if devices != 8:
        return place
    return jnp.where(place < devices // 2, 2 * place, 2 * (devices - 1 - place) + 1)


def attend_kernel(kv_share, unroll, heads_of, q_hbm, ko_hbm, vo_hbm, sign_hbm, kp_any, vp_any, *scratch):
    out_refs, scratch = scratch[: len(heads_of)], scratch[len(heads_of) :]
    homes = [(ref, h) for ref, count in zip(out_refs, heads_of) for h in range(count)]
    q_ref, kv_ref, sign_ref, inner_ref, vt_ref, bar_ref, sem = scratch
    rows, width = q_ref.shape
    heads = width // DH
    scale = math.log2(math.e) / math.sqrt(DH)
    first_head = lax.axis_index("head") * heads
    columns = pl.ds(pl.multiple_of(first_head // kv_share * DH, DH), DH)
    copies = [
        pltpu.make_async_copy(ko_hbm.at[:, columns], kv_ref.at[0], sem.at[0]),
        pltpu.make_async_copy(kp_any.at[:, columns], kv_ref.at[1], sem.at[1]),
        pltpu.make_async_copy(vo_hbm.at[:, columns], kv_ref.at[2], sem.at[2]),
        pltpu.make_async_copy(vp_any.at[:, columns], kv_ref.at[3], sem.at[3]),
        pltpu.make_async_copy(sign_hbm, sign_ref, sem.at[4]),
        pltpu.make_async_copy(q_hbm, q_ref, sem.at[5]),
    ]
    for copy in copies:
        copy.start()
    core = lax.axis_index("tok")
    key_pos = lax.broadcasted_iota(jnp.int32, (rows, rows), 0)
    query_pos = lax.broadcasted_iota(jnp.int32, (rows, rows), 1)
    bar_ref[...] = jnp.where(key_pos <= query_pos, 0.0, -1e30)
    anded = lax.broadcasted_iota(jnp.int32, (DH, DH), 0) & lax.broadcasted_iota(jnp.int32, (DH, DH), 1)
    odd = jnp.zeros_like(anded)
    for level in range(7):
        odd = odd ^ (anded >> level) & 1
    table = (1 - 2 * odd).astype(jnp.float32)
    for copy in copies[2:4]:
        copy.wait()
    vt_ref[:, :rows] = kv_ref[3].astype(jnp.float32).T.astype(jnp.bfloat16)
    vt_ref[:, rows:] = kv_ref[2].astype(jnp.float32).T.astype(jnp.bfloat16)
    for copy in copies[:2] + copies[4:]:
        copy.wait()

    def one(h, earlier):
        q = q_ref[:, pl.ds(pl.multiple_of(h * DH, DH), DH)]
        own = nt_dot(kv_ref[0], q) + bar_ref[...]
        top = jnp.max(own, axis=0, keepdims=True)
        if earlier:
            before = nt_dot(kv_ref[1], q)
            top = jnp.maximum(top, jnp.max(before, axis=0, keepdims=True))
        weights = jnp.exp2((own - top) * scale)
        total = jnp.sum(weights, axis=0, keepdims=True)
        attended = jnp.dot(vt_ref[:, rows:], weights.astype(jnp.bfloat16), preferred_element_type=jnp.float32)
        if earlier:
            weights = jnp.exp2((before - top) * scale)
            total += jnp.sum(weights, axis=0, keepdims=True)
            attended += jnp.dot(vt_ref[:, :rows], weights.astype(jnp.bfloat16), preferred_element_type=jnp.float32)
        attended = attended * (1.0 / total)
        coarse = attended.astype(jnp.bfloat16)
        fine = (attended - coarse.astype(jnp.float32)).astype(jnp.bfloat16)
        signs = (1 - 2 * sign_ref[pl.ds(first_head + h, 1), :]).astype(jnp.float32)
        turn = (table * signs).astype(jnp.bfloat16)
        inner = jnp.dot(turn, coarse, preferred_element_type=jnp.float32) + jnp.dot(
            turn, fine, preferred_element_type=jnp.float32
        )
        inner_ref[h] = (inner * (1.0 / math.sqrt(DH))).astype(jnp.bfloat16)

    unroll = math.gcd(heads, unroll)

    def every(earlier):
        @pl.loop(0, heads // unroll)
        def _(step):
            for u in range(unroll):
                one(step * unroll + u, earlier)

    pl.when(core > 0)(lambda: every(True))
    pl.when(core == 0)(lambda: every(False))

    shrink = 1.0 / math.sqrt(heads)

    @pl.loop(0, DH // 16)
    def _(block):
        band = pl.ds(pl.multiple_of(block * 16, 16), 16)
        for lane in range(0, rows, 128):
            tiles = [inner_ref[h, band, lane : lane + 128].astype(jnp.float32) for h in range(heads)]
            for h, tile in enumerate(butterfly(tiles)):
                out_ref, slot = homes[h]
                at = pl.ds(pl.multiple_of(slot * DH + block * 16, 16), 16)
                out_ref[at, lane : lane + 128] = (tile * shrink).astype(jnp.bfloat16)


def attend(heads_of, queries, own_keys, own_values, signs, prev_keys, prev_values):
    rows, width = queries.shape
    kv_share = HEADS // (own_keys.shape[1] // DH)
    heads = width // DH
    hbm, anywhere = pl.BlockSpec(memory_space=pltpu.HBM), pl.BlockSpec(memory_space=pl.ANY)
    return pl.pallas_call(
        functools.partial(attend_kernel, kv_share, ATTEND_UNROLL, heads_of),
        in_specs=[hbm] * 4 + [anywhere] * 2,
        out_specs=[pl.BlockSpec(memory_space=pltpu.VMEM)] * len(heads_of),
        scratch_shapes=[
            pltpu.VMEM((rows, width), jnp.bfloat16),
            pltpu.VMEM((4, rows, DH), jnp.bfloat16),
            pltpu.VMEM((HEADS, DH), jnp.int32),
            pltpu.VMEM((heads, DH, rows), jnp.bfloat16),
            pltpu.VMEM((DH, 2 * rows), jnp.bfloat16),
            pltpu.VMEM((rows, rows), jnp.float32),
            pltpu.SemaphoreType.DMA((6,)),
        ],
        out_shape=[jax.ShapeDtypeStruct((count * DH, rows), jnp.bfloat16) for count in heads_of],
        compiler_params=pltpu.CompilerParams(vmem_limit_bytes=60 * MIB),
        cost_estimate=pl.CostEstimate(flops=20000000000, bytes_accessed=1024, transcendentals=0),
        name="attend",
    )(queries, own_keys, own_values, signs, prev_keys, prev_values)


def mix_kernel(devices, scale, *refs):
    count = devices + 1
    pieces, (keep_ref, send_ref, held, sem) = refs[:count], refs[count:]
    rows = keep_ref.shape[1]
    lanes = keep_ref.shape[2]
    half = devices // 2
    head, core = lax.axis_index("head"), lax.axis_index("tok")
    place = ring_place(head, devices)
    shifts = [0] + [shift for step in range(1, half) for shift in (devices - step, step)] + [half]
    slots = [ring_device(lax.rem(place + shift, devices), devices) for shift in shifts]
    copies = []
    for p, piece in enumerate(pieces):
        if p == 0:
            source, target = piece, held.at[slots[0]]
        elif p < devices - 1:
            source, target = piece, held.at[slots[p]]
        else:
            part = (p - (devices - 1)) * (rows // 2)
            source, target = piece, held.at[slots[devices - 1], pl.ds(part, rows // 2), :]
        copies.append(pltpu.make_async_copy(source, target, sem.at[p]))
    for copy in copies:
        copy.start()
    for copy in copies:
        copy.wait()
    flip = jnp.where(core > 0, -1.0, 1.0).astype(jnp.float32)
    shrink = 1.0 / math.sqrt(devices)
    in_keep = (head // half) == core
    own_slot = lax.rem(head, half)

    @pl.loop(0, rows // 16)
    def _(block):
        band = pl.ds(pl.multiple_of(block * 16, 16), 16)
        for lane in range(0, lanes, 128):
            span = slice(lane, lane + 128)
            tiles = [held[d, band, span].astype(jnp.float32) for d in range(devices)]
            flipped = [tiles[d + half] * flip for d in range(half)]
            stay = butterfly([tiles[d] + flipped[d] for d in range(half)])
            leave = butterfly([tiles[d] - flipped[d] for d in range(half)])
            for d in range(half):
                keep_ref[d, band, span] = (stay[d] * shrink).astype(jnp.bfloat16)
                send_ref[d, band, span] = (leave[d] * shrink).astype(jnp.bfloat16)

    @pl.when(in_keep)
    def _():
        strip = (keep_ref[own_slot] * scale).astype(jnp.bfloat16)
        keep_ref[half] = strip
        send_ref[half] = strip

    @pl.when(jnp.logical_not(in_keep))
    def _():
        strip = (send_ref[own_slot] * scale).astype(jnp.bfloat16)
        keep_ref[half] = strip
        send_ref[half] = strip


def mix(devices, scale, own, pieces):
    rows, lanes = own.shape
    half = devices // 2
    shape = (half + 1, rows, lanes)
    return pl.pallas_call(
        functools.partial(mix_kernel, devices, scale),
        in_specs=[pl.BlockSpec(memory_space=pl.ANY)] * (devices + 1),
        out_specs=[pl.BlockSpec(memory_space=pltpu.VMEM)] * 2,
        scratch_shapes=[
            pltpu.VMEM((devices, rows, lanes), jnp.bfloat16),
            pltpu.SemaphoreType.DMA((devices + 1,)),
        ],
        out_shape=[jax.ShapeDtypeStruct(shape, jnp.bfloat16)] * 2,
        compiler_params=pltpu.CompilerParams(vmem_limit_bytes=24 * MIB),
        cost_estimate=pl.CostEstimate(flops=20000000000, bytes_accessed=1024, transcendentals=0),
        name="mix",
    )(own, *pieces)


def gram_kernel(starts, sizes, chunk, aliased, *refs):
    refs = list(refs)
    take = lambda n: [refs.pop(0) for _ in range(n)]
    if aliased:
        take(1)
    keeps, recvs = take(chunk + 1), take(chunk + 1)
    half = keeps[0].shape[0] - 1
    (out_ref,) = take(1)
    wide, sem = take(2)
    tall = take(1)[0] if chunk else None
    r, steps = pl.program_id(0), pl.num_programs(0)
    slot = lax.rem(r, 2)
    first, size = starts[chunk], sizes[chunk]

    def wide_copy(at, s):
        return pltpu.make_async_copy(
            wide.at[s], out_ref.at[at, pl.ds(first, size), pl.ds(0, first + size)], sem.at[0, s]
        )

    def tall_copy(at, s):
        return pltpu.make_async_copy(
            tall.at[s], out_ref.at[at, pl.ds(0, first), pl.ds(first, size)], sem.at[1, s]
        )

    @pl.when(r >= 2)
    def _():
        wide_copy(r - 2, slot).wait()
        if chunk:
            tall_copy(r - 2, slot).wait()

    def block(up, across, target, top, left):
        height, width = sizes[up], sizes[across]
        tile_m, tile_n = math.gcd(height, 1024), math.gcd(width, 256)
        for i in range(0, height, tile_m):
            rows, rows_other = keeps[up][r, i : i + tile_m, :], recvs[up][r, i : i + tile_m, :]
            for k in range(0, width, tile_n):
                total = nt_dot(rows, keeps[across][half, k : k + tile_n, :])
                total += nt_dot(rows_other, recvs[across][half, k : k + tile_n, :])
                target[slot, top + i : top + i + tile_m, left + k : left + k + tile_n] = total.astype(jnp.bfloat16)

    for c in range(chunk + 1):
        block(chunk, c, wide, 0, starts[c])
    wide_copy(r, slot).start()
    for c in range(chunk):
        block(c, chunk, tall, starts[c], 0)
    if chunk:
        tall_copy(r, slot).start()

    @pl.when(r == steps - 1)
    def _():
        for back in (1, 0):
            at = r - back
            wide_copy(at, lax.rem(at, 2)).wait()
            if chunk:
                tall_copy(at, lax.rem(at, 2)).wait()


def gram(out, keeps, recvs, starts, sizes, chunk, shape):
    half = keeps[0].shape[0] - 1
    lanes = keeps[0].shape[2]
    first, size = starts[chunk], sizes[chunk]
    aliased = out is not None
    anywhere = pl.BlockSpec(memory_space=pl.ANY)
    scratch = [pltpu.VMEM((2, size, first + size), jnp.bfloat16), pltpu.SemaphoreType.DMA((2, 2))]
    if chunk:
        scratch.append(pltpu.VMEM((2, first, size), jnp.bfloat16))
    area = half * (size * (first + size) + first * size)
    return pl.pallas_call(
        functools.partial(gram_kernel, starts, sizes, chunk, aliased),
        grid=(half,),
        in_specs=([anywhere] if aliased else []) + [pl.BlockSpec(memory_space=pltpu.VMEM)] * (2 * chunk + 2),
        out_specs=anywhere,
        out_shape=jax.ShapeDtypeStruct(shape, jnp.bfloat16),
        scratch_shapes=scratch,
        input_output_aliases={0: 0} if aliased else {},
        compiler_params=pltpu.CompilerParams(vmem_limit_bytes=40 * MIB),
        cost_estimate=pl.CostEstimate(flops=20000000000, bytes_accessed=1024, transcendentals=0),
        name=f"gram{chunk}",
    )(*(([out] if aliased else []) + keeps + recvs))


PLANS = {(16, 4): ([4, 4, 4, 4], [0,1,0,1,0,2,1,0,2,1,3,2,3,2,3,3])}


def plan(local_heads, hops):
    if (local_heads, hops) in PLANS:
        return PLANS[local_heads, hops]
    done = [0] * local_heads
    sequence = []
    while min(done) < hops:
        last = sequence[-1] if sequence else -1
        ready = [c for c in range(local_heads) if done[c] < hops]
        pick = next((c for c in ready if c != last), ready[0])
        done[pick] += 1
        sequence.append(pick)
    return [1] * local_heads, sequence


def after(values, *others):
    return lax.optimization_barrier((tuple(values), others))[0]


def local(devices, queries, key_rows, values, sign_bits):
    rows, width = queries.shape
    tok_count = lax.axis_size("tok")
    half = devices // 2
    order = list(range(devices))
    if devices == 8:
        order = order[0::2] + order[:0:-2]
    forward = [(order[i], order[(i + 1) % devices]) for i in range(devices)]
    backward = [(b, a) for a, b in forward]
    prev_keys, prev_values = lax.ppermute((key_rows, values), "tok", [(0, 1)])
    heads_of, sequence = plan(width // DH, half)
    mixed = attend(heads_of, queries, key_rows, values, sign_bits.reshape(HEADS, DH), prev_keys, prev_values)
    sizes = [c * DH for c in heads_of]
    chunks = len(sizes)
    starts = [sum(sizes[:c]) for c in range(chunks)]
    held = [[block, block] for block in mixed]
    pieces = [[] for _ in range(chunks)]
    scale = 2.0 / (rows * tok_count)
    keeps, recvs, out = [None] * chunks, [None] * chunks, None
    landed, due, sends = [], {}, [None] * chunks

    def compute(kind, c, waits):
        nonlocal out
        if kind == "mix":
            own = mixed[c]
            if waits:
                own, pieces[c] = after((own, pieces[c]), *waits)
            keeps[c], sends[c] = mix(devices, scale, own, pieces[c])
            return keeps[c]
        if kind == "swap":
            if waits:
                sends[c] = after((sends[c],), *waits)[0]
            with jax.named_scope(f"swap{c}"):
                recvs[c] = lax.ppermute(sends[c], "tok", [(0, 1), (1, 0)])
            return recvs[c]
        if waits:
            keeps[c] = after((keeps[c],), *waits)[0]
        out = gram(out, keeps[: c + 1], recvs[: c + 1], starts, sizes, c, (half, width, width))
        return out

    pending = []
    for k, c in enumerate(sequence):
        going, coming = held[c]
        if len(pieces[c]) == 2 * (half - 1):
            going, coming = going[: sizes[c] // 2], coming[sizes[c] // 2 :]
        waits = landed[max(0, k - DEPTH - 1) : max(0, k - DEPTH + 1)] + due.pop(k, [])
        if waits:
            going, coming = after((going, coming), *waits)
        with jax.named_scope(f"up{k}c{c}"):
            going = lax.ppermute(going, "head", forward)
        with jax.named_scope(f"down{k}c{c}"):
            coming = lax.ppermute(coming, "head", backward)
        landed.append((going, coming))
        held[c] = [going, coming]
        pieces[c] += [going, coming]
        if len(pieces[c]) == 2 * half:
            for kind, (ready, deadline) in GATES.items():
                pending.append((kind, c, k + ready, k + deadline))
        for task in list(pending):
            kind, which, ready, deadline = task
            if ready == k:
                pending.remove(task)
                due.setdefault(deadline, []).append(compute(kind, which, [landed[k]]))
    for kind, which, _, _ in pending:
        compute(kind, which, [])
    return out.reshape(half * width, width)


def solution(mesh):
    placed = (P(("grp", "tok"), "head"), P(("grp", "tok"), None), P(("grp", "tok"), None), P())
    return jax.shard_map(
        functools.partial(local, mesh.shape["head"]),
        mesh=mesh,
        in_specs=placed,
        out_specs=P(("grp", "tok"), "head"),
        check_vma=False,
    )
```

```python
import functools
import math

import jax
import jax.numpy as jnp
from jax import lax
from jax.experimental import pallas as pl
from jax.experimental.pallas import tpu as pltpu
from jax.sharding import PartitionSpec as P

HEADS = 128
DH = 128
MIB = 1024 * 1024
ATTEND_UNROLL = 8
DEPTH = 3
GATES = {"mix": (1, 4), "swap": (2, 5), "gram": (3, 6)}


def butterfly(tiles):
    if len(tiles) == 1:
        return tiles
    half = len(tiles) // 2
    low = [tiles[i] + tiles[i + half] for i in range(half)]
    high = [tiles[i] - tiles[i + half] for i in range(half)]
    return butterfly(low) + butterfly(high)


def nt_dot(left, right):
    return lax.dot_general(left, right, (((1,), (1,)), ((), ())), preferred_element_type=jnp.float32)


def ring_place(device, devices):
    if devices != 8:
        return device
    upward = device // 2
    return jnp.where(lax.rem(device, 2) == 0, upward, devices - 1 - upward)


def ring_device(place, devices):
    if devices != 8:
        return place
    return jnp.where(place < devices // 2, 2 * place, 2 * (devices - 1 - place) + 1)


def attend_kernel(unroll, heads_of, q_hbm, sign_hbm, own_any, prev_any, *scratch):
    out_refs, scratch = scratch[: len(heads_of)], scratch[len(heads_of) :]
    homes = [(ref, h) for ref, count in zip(out_refs, heads_of) for h in range(count)]
    q_ref, kv_ref, sign_ref, inner_ref, vt_ref, bar_ref, sem = scratch
    rows, width = q_ref.shape
    heads = width // DH
    scale = math.log2(math.e) / math.sqrt(DH)
    first_head = lax.axis_index("head") * heads
    copies = [
        pltpu.make_async_copy(own_any, kv_ref.at[0], sem.at[0]),
        pltpu.make_async_copy(prev_any, kv_ref.at[1], sem.at[1]),
        pltpu.make_async_copy(sign_hbm, sign_ref, sem.at[2]),
        pltpu.make_async_copy(q_hbm, q_ref, sem.at[3]),
    ]
    for copy in copies:
        copy.start()
    core = lax.axis_index("tok")
    key_pos = lax.broadcasted_iota(jnp.int32, (rows, rows), 0)
    query_pos = lax.broadcasted_iota(jnp.int32, (rows, rows), 1)
    bar_ref[...] = jnp.where(key_pos <= query_pos, 0.0, -1e30)
    anded = lax.broadcasted_iota(jnp.int32, (DH, DH), 0) & lax.broadcasted_iota(jnp.int32, (DH, DH), 1)
    odd = jnp.zeros_like(anded)
    for level in range(7):
        odd = odd ^ (anded >> level) & 1
    table = (1 - 2 * odd).astype(jnp.float32)
    for copy in copies[:2]:
        copy.wait()
    vt_ref[:, :rows] = kv_ref[1, :, DH:].astype(jnp.float32).T.astype(jnp.bfloat16)
    vt_ref[:, rows:] = kv_ref[0, :, DH:].astype(jnp.float32).T.astype(jnp.bfloat16)
    for copy in copies[2:]:
        copy.wait()

    def one(h, earlier):
        q = q_ref[:, pl.ds(pl.multiple_of(h * DH, DH), DH)]
        own = nt_dot(kv_ref[0, :, :DH], q) + bar_ref[...]
        top = jnp.max(own, axis=0, keepdims=True)
        if earlier:
            before = nt_dot(kv_ref[1, :, :DH], q)
            top = jnp.maximum(top, jnp.max(before, axis=0, keepdims=True))
        weights = jnp.exp2((own - top) * scale)
        total = jnp.sum(weights, axis=0, keepdims=True)
        attended = jnp.dot(vt_ref[:, rows:], weights.astype(jnp.bfloat16), preferred_element_type=jnp.float32)
        if earlier:
            weights = jnp.exp2((before - top) * scale)
            total += jnp.sum(weights, axis=0, keepdims=True)
            attended += jnp.dot(vt_ref[:, :rows], weights.astype(jnp.bfloat16), preferred_element_type=jnp.float32)
        attended = attended * (1.0 / total)
        coarse = attended.astype(jnp.bfloat16)
        fine = (attended - coarse.astype(jnp.float32)).astype(jnp.bfloat16)
        signs = (1 - 2 * sign_ref[pl.ds(first_head + h, 1), :]).astype(jnp.float32)
        turn = (table * signs).astype(jnp.bfloat16)
        inner = jnp.dot(turn, coarse, preferred_element_type=jnp.float32) + jnp.dot(
            turn, fine, preferred_element_type=jnp.float32
        )
        inner_ref[h] = (inner * (1.0 / math.sqrt(DH))).astype(jnp.bfloat16)

    unroll = math.gcd(heads, unroll)

    def every(earlier):
        @pl.loop(0, heads // unroll)
        def _(step):
            for u in range(unroll):
                one(step * unroll + u, earlier)

    pl.when(core > 0)(lambda: every(True))
    pl.when(core == 0)(lambda: every(False))

    shrink = 1.0 / math.sqrt(heads)

    @pl.loop(0, DH // 16)
    def _(block):
        band = pl.ds(pl.multiple_of(block * 16, 16), 16)
        for lane in range(0, rows, 128):
            tiles = [inner_ref[h, band, lane : lane + 128].astype(jnp.float32) for h in range(heads)]
            for h, tile in enumerate(butterfly(tiles)):
                out_ref, slot = homes[h]
                at = pl.ds(pl.multiple_of(slot * DH + block * 16, 16), 16)
                out_ref[at, lane : lane + 128] = (tile * shrink).astype(jnp.bfloat16)


def attend(heads_of, queries, signs, own, prev):
    rows, width = queries.shape
    heads = width // DH
    hbm, anywhere = pl.BlockSpec(memory_space=pltpu.HBM), pl.BlockSpec(memory_space=pl.ANY)
    return pl.pallas_call(
        functools.partial(attend_kernel, ATTEND_UNROLL, heads_of),
        in_specs=[hbm] * 2 + [anywhere] * 2,
        out_specs=[pl.BlockSpec(memory_space=pltpu.VMEM)] * len(heads_of),
        scratch_shapes=[
            pltpu.VMEM((rows, width), jnp.bfloat16),
            pltpu.VMEM((2, rows, 2 * DH), jnp.bfloat16),
            pltpu.VMEM((HEADS, DH), jnp.int32),
            pltpu.VMEM((heads, DH, rows), jnp.bfloat16),
            pltpu.VMEM((DH, 2 * rows), jnp.bfloat16),
            pltpu.VMEM((rows, rows), jnp.float32),
            pltpu.SemaphoreType.DMA((4,)),
        ],
        out_shape=[jax.ShapeDtypeStruct((count * DH, rows), jnp.bfloat16) for count in heads_of],
        compiler_params=pltpu.CompilerParams(vmem_limit_bytes=60 * MIB),
        cost_estimate=pl.CostEstimate(flops=20000000000, bytes_accessed=1024, transcendentals=0),
        name="attend",
    )(queries, signs, own, prev)


def mix_kernel(devices, scale, *refs):
    count = devices + 1
    pieces, (keep_ref, send_ref, held, sem) = refs[:count], refs[count:]
    rows = keep_ref.shape[1]
    lanes = keep_ref.shape[2]
    half = devices // 2
    head, core = lax.axis_index("head"), lax.axis_index("tok")
    place = ring_place(head, devices)
    shifts = [0] + [shift for step in range(1, half) for shift in (devices - step, step)] + [half]
    slots = [ring_device(lax.rem(place + shift, devices), devices) for shift in shifts]
    copies = []
    for p, piece in enumerate(pieces):
        if p == 0:
            source, target = piece, held.at[slots[0]]
        elif p < devices - 1:
            source, target = piece, held.at[slots[p]]
        else:
            part = (p - (devices - 1)) * (rows // 2)
            source, target = piece, held.at[slots[devices - 1], pl.ds(part, rows // 2), :]
        copies.append(pltpu.make_async_copy(source, target, sem.at[p]))
    for copy in copies:
        copy.start()
    for copy in copies:
        copy.wait()
    flip = jnp.where(core > 0, -1.0, 1.0).astype(jnp.float32)
    shrink = 1.0 / math.sqrt(devices)
    in_keep = (head // half) == core
    own_slot = lax.rem(head, half)

    @pl.loop(0, rows // 16)
    def _(block):
        band = pl.ds(pl.multiple_of(block * 16, 16), 16)
        for lane in range(0, lanes, 128):
            span = slice(lane, lane + 128)
            tiles = [held[d, band, span].astype(jnp.float32) for d in range(devices)]
            flipped = [tiles[d + half] * flip for d in range(half)]
            stay = butterfly([tiles[d] + flipped[d] for d in range(half)])
            leave = butterfly([tiles[d] - flipped[d] for d in range(half)])
            for d in range(half):
                keep_ref[d, band, span] = (stay[d] * shrink).astype(jnp.bfloat16)
                send_ref[d, band, span] = (leave[d] * shrink).astype(jnp.bfloat16)

    @pl.when(in_keep)
    def _():
        strip = (keep_ref[own_slot] * scale).astype(jnp.bfloat16)
        keep_ref[half] = strip
        send_ref[half] = strip

    @pl.when(jnp.logical_not(in_keep))
    def _():
        strip = (send_ref[own_slot] * scale).astype(jnp.bfloat16)
        keep_ref[half] = strip
        send_ref[half] = strip


def mix(devices, scale, own, pieces):
    rows, lanes = own.shape
    half = devices // 2
    shape = (half + 1, rows, lanes)
    return pl.pallas_call(
        functools.partial(mix_kernel, devices, scale),
        in_specs=[pl.BlockSpec(memory_space=pl.ANY)] * (devices + 1),
        out_specs=[pl.BlockSpec(memory_space=pltpu.VMEM)] * 2,
        scratch_shapes=[
            pltpu.VMEM((devices, rows, lanes), jnp.bfloat16),
            pltpu.SemaphoreType.DMA((devices + 1,)),
        ],
        out_shape=[jax.ShapeDtypeStruct(shape, jnp.bfloat16)] * 2,
        compiler_params=pltpu.CompilerParams(vmem_limit_bytes=24 * MIB),
        cost_estimate=pl.CostEstimate(flops=20000000000, bytes_accessed=1024, transcendentals=0),
        name="mix",
    )(own, *pieces)


def gram_kernel(starts, sizes, chunk, aliased, *refs):
    refs = list(refs)
    take = lambda n: [refs.pop(0) for _ in range(n)]
    if aliased:
        take(1)
    keeps, recvs = take(chunk + 1), take(chunk + 1)
    half = keeps[0].shape[0] - 1
    (out_ref,) = take(1)
    wide, sem = take(2)
    tall = take(1)[0] if chunk else None
    r, steps = pl.program_id(0), pl.num_programs(0)
    slot = lax.rem(r, 2)
    first, size = starts[chunk], sizes[chunk]

    def wide_copy(at, s):
        return pltpu.make_async_copy(
            wide.at[s], out_ref.at[at, pl.ds(first, size), pl.ds(0, first + size)], sem.at[0, s]
        )

    def tall_copy(at, s):
        return pltpu.make_async_copy(
            tall.at[s], out_ref.at[at, pl.ds(0, first), pl.ds(first, size)], sem.at[1, s]
        )

    @pl.when(r >= 2)
    def _():
        wide_copy(r - 2, slot).wait()
        if chunk:
            tall_copy(r - 2, slot).wait()

    def block(up, across, target, top, left):
        height, width = sizes[up], sizes[across]
        tile_m, tile_n = math.gcd(height, 1024), math.gcd(width, 256)
        for i in range(0, height, tile_m):
            rows, rows_other = keeps[up][r, i : i + tile_m, :], recvs[up][r, i : i + tile_m, :]
            for k in range(0, width, tile_n):
                total = nt_dot(rows, keeps[across][half, k : k + tile_n, :])
                total += nt_dot(rows_other, recvs[across][half, k : k + tile_n, :])
                target[slot, top + i : top + i + tile_m, left + k : left + k + tile_n] = total.astype(jnp.bfloat16)

    for c in range(chunk + 1):
        block(chunk, c, wide, 0, starts[c])
    wide_copy(r, slot).start()
    for c in range(chunk):
        block(c, chunk, tall, starts[c], 0)
    if chunk:
        tall_copy(r, slot).start()

    @pl.when(r == steps - 1)
    def _():
        for back in (1, 0):
            at = r - back
            wide_copy(at, lax.rem(at, 2)).wait()
            if chunk:
                tall_copy(at, lax.rem(at, 2)).wait()


def gram(out, keeps, recvs, starts, sizes, chunk, shape):
    half = keeps[0].shape[0] - 1
    lanes = keeps[0].shape[2]
    first, size = starts[chunk], sizes[chunk]
    aliased = out is not None
    anywhere = pl.BlockSpec(memory_space=pl.ANY)
    scratch = [pltpu.VMEM((2, size, first + size), jnp.bfloat16), pltpu.SemaphoreType.DMA((2, 2))]
    if chunk:
        scratch.append(pltpu.VMEM((2, first, size), jnp.bfloat16))
    area = half * (size * (first + size) + first * size)
    return pl.pallas_call(
        functools.partial(gram_kernel, starts, sizes, chunk, aliased),
        grid=(half,),
        in_specs=([anywhere] if aliased else []) + [pl.BlockSpec(memory_space=pltpu.VMEM)] * (2 * chunk + 2),
        out_specs=anywhere,
        out_shape=jax.ShapeDtypeStruct(shape, jnp.bfloat16),
        scratch_shapes=scratch,
        input_output_aliases={0: 0} if aliased else {},
        compiler_params=pltpu.CompilerParams(vmem_limit_bytes=40 * MIB),
        cost_estimate=pl.CostEstimate(flops=20000000000, bytes_accessed=1024, transcendentals=0),
        name=f"gram{chunk}",
    )(*(([out] if aliased else []) + keeps + recvs))


PLANS = {(16, 4): ([4, 4, 4, 4], [0, 1, 0, 1, 2, 0, 1, 2, 0, 1, 3, 2, 3, 2, 3, 3])}


def plan(local_heads, hops):
    if (local_heads, hops) in PLANS:
        return PLANS[local_heads, hops]
    done = [0] * local_heads
    sequence = []
    while min(done) < hops:
        last = sequence[-1] if sequence else -1
        ready = [c for c in range(local_heads) if done[c] < hops]
        pick = next((c for c in ready if c != last), ready[0])
        done[pick] += 1
        sequence.append(pick)
    return [1] * local_heads, sequence


def after(values, *others):
    return lax.optimization_barrier((tuple(values), others))[0]


def local(devices, queries, key_rows, values, sign_bits):
    rows, width = queries.shape
    tok_count = lax.axis_size("tok")
    half = devices // 2
    order = list(range(devices))
    if devices == 8:
        order = order[0::2] + order[:0:-2]
    forward = [(order[i], order[(i + 1) % devices]) for i in range(devices)]
    backward = [(b, a) for a, b in forward]
    kv_share = HEADS // (key_rows.shape[1] // DH)
    first = lax.axis_index("head") * (width // DH) // kv_share * DH
    own = jnp.concatenate([lax.dynamic_slice_in_dim(x, first, DH, 1) for x in (key_rows, values)], 1)
    prev = lax.ppermute(own, "tok", [(0, 1)])
    heads_of, sequence = plan(width // DH, half)
    mixed = attend(heads_of, queries, sign_bits.reshape(HEADS, DH), own, prev)
    sizes = [c * DH for c in heads_of]
    chunks = len(sizes)
    starts = [sum(sizes[:c]) for c in range(chunks)]
    held = [[block, block] for block in mixed]
    pieces = [[] for _ in range(chunks)]
    scale = 2.0 / (rows * tok_count)
    keeps, recvs, out = [None] * chunks, [None] * chunks, None
    landed, due, sends = [], {}, [None] * chunks

    def compute(kind, c, waits):
        nonlocal out
        if kind == "mix":
            own = mixed[c]
            if waits:
                own, pieces[c] = after((own, pieces[c]), *waits)
            keeps[c], sends[c] = mix(devices, scale, own, pieces[c])
            return keeps[c]
        if kind == "swap":
            if waits:
                sends[c] = after((sends[c],), *waits)[0]
            with jax.named_scope(f"swap{c}"):
                recvs[c] = lax.ppermute(sends[c], "tok", [(0, 1), (1, 0)])
            return recvs[c]
        if waits:
            keeps[c] = after((keeps[c],), *waits)[0]
        out = gram(out, keeps[: c + 1], recvs[: c + 1], starts, sizes, c, (half, width, width))
        return out

    pending = []
    for k, c in enumerate(sequence):
        going, coming = held[c]
        if len(pieces[c]) == 2 * (half - 1):
            going, coming = going[: sizes[c] // 2], coming[sizes[c] // 2 :]
        waits = landed[max(0, k - DEPTH - 1) : max(0, k - DEPTH + 1)] + due.pop(k, [])
        if waits:
            going, coming = after((going, coming), *waits)
        with jax.named_scope(f"up{k}c{c}"):
            going = lax.ppermute(going, "head", forward)
        with jax.named_scope(f"down{k}c{c}"):
            coming = lax.ppermute(coming, "head", backward)
        landed.append((going, coming))
        held[c] = [going, coming]
        pieces[c] += [going, coming]
        if len(pieces[c]) == 2 * half:
            for kind, (ready, deadline) in GATES.items():
                pending.append((kind, c, k + ready, k + deadline))
        for task in list(pending):
            kind, which, ready, deadline = task
            if ready == k:
                pending.remove(task)
                due.setdefault(deadline, []).append(compute(kind, which, [landed[k]]))
    for kind, which, _, _ in pending:
        compute(kind, which, [])
    return out.reshape(half * width, width)


def solution(mesh):
    placed = (P(("grp", "tok"), "head"), P(("grp", "tok"), None), P(("grp", "tok"), None), P())
    return jax.shard_map(
        functools.partial(local, mesh.shape["head"]),
        mesh=mesh,
        in_specs=placed,
        out_specs=P(("grp", "tok"), "head"),
        check_vma=False,
    )
```

```python
import functools
import math

import jax
import jax.numpy as jnp
from jax import lax
from jax.experimental import pallas as pl
from jax.experimental.pallas import tpu as pltpu
from jax.sharding import PartitionSpec as P

HEADS = 128
DH = 128
MIB = 1024 * 1024
ATTEND_UNROLL = 8
DEPTH = 3
GATES = {"mix": (1, 4), "swap": (2, 5), "gram": (3, 6)}


def butterfly(tiles):
    if len(tiles) == 1:
        return tiles
    half = len(tiles) // 2
    low = [tiles[i] + tiles[i + half] for i in range(half)]
    high = [tiles[i] - tiles[i + half] for i in range(half)]
    return butterfly(low) + butterfly(high)


def nt_dot(left, right):
    return lax.dot_general(left, right, (((1,), (1,)), ((), ())), preferred_element_type=jnp.float32)


def ring_place(device, devices):
    if devices != 8:
        return device
    upward = device // 2
    return jnp.where(lax.rem(device, 2) == 0, upward, devices - 1 - upward)


def ring_device(place, devices):
    if devices != 8:
        return place
    return jnp.where(place < devices // 2, 2 * place, 2 * (devices - 1 - place) + 1)


def attend_kernel(unroll, heads_of, q_hbm, sign_hbm, own_any, prev_any, *scratch):
    out_refs, scratch = scratch[: len(heads_of)], scratch[len(heads_of) :]
    homes = [(ref, h) for ref, count in zip(out_refs, heads_of) for h in range(count)]
    q_ref, kv_ref, sign_ref, inner_ref, vt_ref, bar_ref, sem = scratch
    rows, width = q_ref.shape
    heads = width // DH
    scale = math.log2(math.e) / math.sqrt(DH)
    first_head = lax.axis_index("head") * heads
    copies = [
        pltpu.make_async_copy(own_any, kv_ref.at[0], sem.at[0]),
        pltpu.make_async_copy(prev_any, kv_ref.at[1], sem.at[1]),
        pltpu.make_async_copy(sign_hbm, sign_ref, sem.at[2]),
        pltpu.make_async_copy(q_hbm, q_ref, sem.at[3]),
    ]
    for copy in copies:
        copy.start()
    core = lax.axis_index("tok")
    key_pos = lax.broadcasted_iota(jnp.int32, (rows, rows), 0)
    query_pos = lax.broadcasted_iota(jnp.int32, (rows, rows), 1)
    bar_ref[...] = jnp.where(key_pos <= query_pos, 0.0, -1e30)
    anded = lax.broadcasted_iota(jnp.int32, (DH, DH), 0) & lax.broadcasted_iota(jnp.int32, (DH, DH), 1)
    odd = jnp.zeros_like(anded)
    for level in range(7):
        odd = odd ^ (anded >> level) & 1
    table = (1 - 2 * odd).astype(jnp.float32)
    for copy in copies[:2]:
        copy.wait()
    vt_ref[:, :rows] = kv_ref[1, :, DH:].astype(jnp.float32).T.astype(jnp.bfloat16)
    vt_ref[:, rows:] = kv_ref[0, :, DH:].astype(jnp.float32).T.astype(jnp.bfloat16)
    for copy in copies[2:]:
        copy.wait()

    def one(h, earlier):
        q = q_ref[:, pl.ds(pl.multiple_of(h * DH, DH), DH)]
        own = nt_dot(kv_ref[0, :, :DH], q) + bar_ref[...]
        top = jnp.max(own, axis=0, keepdims=True)
        if earlier:
            before = nt_dot(kv_ref[1, :, :DH], q)
            top = jnp.maximum(top, jnp.max(before, axis=0, keepdims=True))
        weights = jnp.exp2((own - top) * scale)
        total = jnp.sum(weights, axis=0, keepdims=True)
        attended = jnp.dot(vt_ref[:, rows:], weights.astype(jnp.bfloat16), preferred_element_type=jnp.float32)
        if earlier:
            weights = jnp.exp2((before - top) * scale)
            total += jnp.sum(weights, axis=0, keepdims=True)
            attended += jnp.dot(vt_ref[:, :rows], weights.astype(jnp.bfloat16), preferred_element_type=jnp.float32)
        attended = attended * (1.0 / total)
        coarse = attended.astype(jnp.bfloat16)
        fine = (attended - coarse.astype(jnp.float32)).astype(jnp.bfloat16)
        signs = (1 - 2 * sign_ref[pl.ds(first_head + h, 1), :]).astype(jnp.float32)
        turn = (table * signs).astype(jnp.bfloat16)
        inner = jnp.dot(turn, coarse, preferred_element_type=jnp.float32) + jnp.dot(
            turn, fine, preferred_element_type=jnp.float32
        )
        inner_ref[h] = (inner * (1.0 / math.sqrt(DH))).astype(jnp.bfloat16)

    unroll = math.gcd(heads, unroll)

    def every(earlier):
        @pl.loop(0, heads // unroll)
        def _(step):
            for u in range(unroll):
                one(step * unroll + u, earlier)

    pl.when(core > 0)(lambda: every(True))
    pl.when(core == 0)(lambda: every(False))

    shrink = 1.0 / math.sqrt(heads)

    @pl.loop(0, DH // 16)
    def _(block):
        band = pl.ds(pl.multiple_of(block * 16, 16), 16)
        for lane in range(0, rows, 128):
            tiles = [inner_ref[h, band, lane : lane + 128].astype(jnp.float32) for h in range(heads)]
            for h, tile in enumerate(butterfly(tiles)):
                out_ref, slot = homes[h]
                at = pl.ds(pl.multiple_of(slot * DH + block * 16, 16), 16)
                out_ref[at, lane : lane + 128] = (tile * shrink).astype(jnp.bfloat16)


def attend(heads_of, queries, signs, own, prev):
    rows, width = queries.shape
    heads = width // DH
    hbm, anywhere = pl.BlockSpec(memory_space=pltpu.HBM), pl.BlockSpec(memory_space=pl.ANY)
    return pl.pallas_call(
        functools.partial(attend_kernel, ATTEND_UNROLL, heads_of),
        in_specs=[hbm] * 2 + [anywhere] * 2,
        out_specs=[pl.BlockSpec(memory_space=pltpu.VMEM)] * len(heads_of),
        scratch_shapes=[
            pltpu.VMEM((rows, width), jnp.bfloat16),
            pltpu.VMEM((2, rows, 2 * DH), jnp.bfloat16),
            pltpu.VMEM((HEADS, DH), jnp.int32),
            pltpu.VMEM((heads, DH, rows), jnp.bfloat16),
            pltpu.VMEM((DH, 2 * rows), jnp.bfloat16),
            pltpu.VMEM((rows, rows), jnp.float32),
            pltpu.SemaphoreType.DMA((4,)),
        ],
        out_shape=[jax.ShapeDtypeStruct((count * DH, rows), jnp.bfloat16) for count in heads_of],
        compiler_params=pltpu.CompilerParams(vmem_limit_bytes=60 * MIB),
        cost_estimate=pl.CostEstimate(flops=20000000000, bytes_accessed=1024, transcendentals=0),
        name="attend",
    )(queries, signs, own, prev)


def mix_kernel(devices, scale, *refs):
    count = devices + 1
    pieces, (keep_ref, send_ref, held, sem) = refs[:count], refs[count:]
    rows = keep_ref.shape[1]
    lanes = keep_ref.shape[2]
    half = devices // 2
    head, core = lax.axis_index("head"), lax.axis_index("tok")
    place = ring_place(head, devices)
    shifts = [0] + [shift for step in range(1, half) for shift in (devices - step, step)] + [half]
    slots = [ring_device(lax.rem(place + shift, devices), devices) for shift in shifts]
    copies = []
    for p, piece in enumerate(pieces):
        if p == 0:
            source, target = piece, held.at[slots[0]]
        elif p < devices - 1:
            source, target = piece, held.at[slots[p]]
        else:
            part = (p - (devices - 1)) * (rows // 2)
            source, target = piece, held.at[slots[devices - 1], pl.ds(part, rows // 2), :]
        copies.append(pltpu.make_async_copy(source, target, sem.at[p]))
    for copy in copies:
        copy.start()
    for copy in copies:
        copy.wait()
    flip = jnp.where(core > 0, -1.0, 1.0).astype(jnp.float32)
    shrink = 1.0 / math.sqrt(devices)
    in_keep = (head // half) == core
    own_slot = lax.rem(head, half)

    @pl.loop(0, rows // 16)
    def _(block):
        band = pl.ds(pl.multiple_of(block * 16, 16), 16)
        for lane in range(0, lanes, 128):
            span = slice(lane, lane + 128)
            tiles = [held[d, band, span].astype(jnp.float32) for d in range(devices)]
            flipped = [tiles[d + half] * flip for d in range(half)]
            stay = butterfly([tiles[d] + flipped[d] for d in range(half)])
            leave = butterfly([tiles[d] - flipped[d] for d in range(half)])
            for d in range(half):
                keep_ref[d, band, span] = (stay[d] * shrink).astype(jnp.bfloat16)
                send_ref[d, band, span] = (leave[d] * shrink).astype(jnp.bfloat16)

    @pl.when(in_keep)
    def _():
        strip = (keep_ref[own_slot] * scale).astype(jnp.bfloat16)
        keep_ref[half] = strip
        send_ref[half] = strip

    @pl.when(jnp.logical_not(in_keep))
    def _():
        strip = (send_ref[own_slot] * scale).astype(jnp.bfloat16)
        keep_ref[half] = strip
        send_ref[half] = strip


def mix(devices, scale, own, pieces):
    rows, lanes = own.shape
    half = devices // 2
    shape = (half + 1, rows, lanes)
    return pl.pallas_call(
        functools.partial(mix_kernel, devices, scale),
        in_specs=[pl.BlockSpec(memory_space=pl.ANY)] * (devices + 1),
        out_specs=[pl.BlockSpec(memory_space=pltpu.VMEM)] * 2,
        scratch_shapes=[
            pltpu.VMEM((devices, rows, lanes), jnp.bfloat16),
            pltpu.SemaphoreType.DMA((devices + 1,)),
        ],
        out_shape=[jax.ShapeDtypeStruct(shape, jnp.bfloat16)] * 2,
        compiler_params=pltpu.CompilerParams(vmem_limit_bytes=24 * MIB),
        cost_estimate=pl.CostEstimate(flops=20000000000, bytes_accessed=1024, transcendentals=0),
        name="mix",
    )(own, *pieces)


def gram_kernel(starts, sizes, chunk, aliased, *refs):
    refs = list(refs)
    take = lambda n: [refs.pop(0) for _ in range(n)]
    if aliased:
        take(1)
    keeps, recvs = take(chunk + 1), take(chunk + 1)
    half = keeps[0].shape[0] - 1
    (out_ref,) = take(1)
    wide, sem = take(2)
    tall = take(1)[0] if chunk else None
    r, steps = pl.program_id(0), pl.num_programs(0)
    slot = lax.rem(r, 2)
    first, size = starts[chunk], sizes[chunk]

    def wide_copy(at, s):
        return pltpu.make_async_copy(
            wide.at[s], out_ref.at[at, pl.ds(first, size), pl.ds(0, first + size)], sem.at[0, s]
        )

    def tall_copy(at, s):
        return pltpu.make_async_copy(
            tall.at[s], out_ref.at[at, pl.ds(0, first), pl.ds(first, size)], sem.at[1, s]
        )

    @pl.when(r >= 2)
    def _():
        wide_copy(r - 2, slot).wait()
        if chunk:
            tall_copy(r - 2, slot).wait()

    def block(up, across, target, top, left):
        height, width = sizes[up], sizes[across]
        tile_m, tile_n = math.gcd(height, 1024), math.gcd(width, 256)
        for i in range(0, height, tile_m):
            rows, rows_other = keeps[up][r, i : i + tile_m, :], recvs[up][r, i : i + tile_m, :]
            for k in range(0, width, tile_n):
                total = nt_dot(rows, keeps[across][half, k : k + tile_n, :])
                total += nt_dot(rows_other, recvs[across][half, k : k + tile_n, :])
                target[slot, top + i : top + i + tile_m, left + k : left + k + tile_n] = total.astype(jnp.bfloat16)

    for c in range(chunk + 1):
        block(chunk, c, wide, 0, starts[c])
    wide_copy(r, slot).start()
    for c in range(chunk):
        block(c, chunk, tall, starts[c], 0)
    if chunk:
        tall_copy(r, slot).start()

    @pl.when(r == steps - 1)
    def _():
        for back in (1, 0):
            at = r - back
            wide_copy(at, lax.rem(at, 2)).wait()
            if chunk:
                tall_copy(at, lax.rem(at, 2)).wait()


def gram(out, keeps, recvs, starts, sizes, chunk, shape):
    half = keeps[0].shape[0] - 1
    lanes = keeps[0].shape[2]
    first, size = starts[chunk], sizes[chunk]
    aliased = out is not None
    anywhere = pl.BlockSpec(memory_space=pl.ANY)
    scratch = [pltpu.VMEM((2, size, first + size), jnp.bfloat16), pltpu.SemaphoreType.DMA((2, 2))]
    if chunk:
        scratch.append(pltpu.VMEM((2, first, size), jnp.bfloat16))
    area = half * (size * (first + size) + first * size)
    return pl.pallas_call(
        functools.partial(gram_kernel, starts, sizes, chunk, aliased),
        grid=(half,),
        in_specs=([anywhere] if aliased else []) + [pl.BlockSpec(memory_space=pltpu.VMEM)] * (2 * chunk + 2),
        out_specs=anywhere,
        out_shape=jax.ShapeDtypeStruct(shape, jnp.bfloat16),
        scratch_shapes=scratch,
        input_output_aliases={0: 0} if aliased else {},
        compiler_params=pltpu.CompilerParams(vmem_limit_bytes=40 * MIB),
        cost_estimate=pl.CostEstimate(flops=20000000000, bytes_accessed=1024, transcendentals=0),
        name=f"gram{chunk}",
    )(*(([out] if aliased else []) + keeps + recvs))


PLANS = {(16, 4): ([4, 4, 4, 4], [0, 1, 0, 1, 2, 0, 1, 0, 2, 1, 3, 2, 3, 2, 3, 3])}


def plan(local_heads, hops):
    if (local_heads, hops) in PLANS:
        return PLANS[local_heads, hops]
    done = [0] * local_heads
    sequence = []
    while min(done) < hops:
        last = sequence[-1] if sequence else -1
        ready = [c for c in range(local_heads) if done[c] < hops]
        pick = next((c for c in ready if c != last), ready[0])
        done[pick] += 1
        sequence.append(pick)
    return [1] * local_heads, sequence


def after(values, *others):
    return lax.optimization_barrier((tuple(values), others))[0]


def local(devices, queries, key_rows, values, sign_bits):
    rows, width = queries.shape
    tok_count = lax.axis_size("tok")
    half = devices // 2
    order = list(range(devices))
    if devices == 8:
        order = order[0::2] + order[:0:-2]
    forward = [(order[i], order[(i + 1) % devices]) for i in range(devices)]
    backward = [(b, a) for a, b in forward]
    kv_share = HEADS // (key_rows.shape[1] // DH)
    first = lax.axis_index("head") * (width // DH) // kv_share * DH
    own = jnp.concatenate([lax.dynamic_slice_in_dim(x, first, DH, 1) for x in (key_rows, values)], 1)
    prev = lax.ppermute(own, "tok", [(0, 1)])
    heads_of, sequence = plan(width // DH, half)
    mixed = attend(heads_of, queries, sign_bits.reshape(HEADS, DH), own, prev)
    sizes = [c * DH for c in heads_of]
    chunks = len(sizes)
    starts = [sum(sizes[:c]) for c in range(chunks)]
    held = [[block, block] for block in mixed]
    pieces = [[] for _ in range(chunks)]
    scale = 2.0 / (rows * tok_count)
    keeps, recvs, out = [None] * chunks, [None] * chunks, None
    landed, due, sends = [], {}, [None] * chunks

    def compute(kind, c, waits):
        nonlocal out
        if kind == "mix":
            own = mixed[c]
            if waits:
                own, pieces[c] = after((own, pieces[c]), *waits)
            keeps[c], sends[c] = mix(devices, scale, own, pieces[c])
            return keeps[c]
        if kind == "swap":
            if waits:
                sends[c] = after((sends[c],), *waits)[0]
            with jax.named_scope(f"swap{c}"):
                recvs[c] = lax.ppermute(sends[c], "tok", [(0, 1), (1, 0)])
            return recvs[c]
        if waits:
            keeps[c] = after((keeps[c],), *waits)[0]
        out = gram(out, keeps[: c + 1], recvs[: c + 1], starts, sizes, c, (half, width, width))
        return out

    pending = []
    for k, c in enumerate(sequence):
        going, coming = held[c]
        if len(pieces[c]) == 2 * (half - 1):
            going, coming = going[: sizes[c] // 2], coming[sizes[c] // 2 :]
        waits = landed[max(0, k - DEPTH - 1) : max(0, k - DEPTH + 1)] + due.pop(k, [])
        if waits:
            going, coming = after((going, coming), *waits)
        with jax.named_scope(f"up{k}c{c}"):
            going = lax.ppermute(going, "head", forward)
        with jax.named_scope(f"down{k}c{c}"):
            coming = lax.ppermute(coming, "head", backward)
        landed.append((going, coming))
        held[c] = [going, coming]
        pieces[c] += [going, coming]
        if len(pieces[c]) == 2 * half:
            for kind, (ready, deadline) in GATES.items():
                pending.append((kind, c, k + ready, k + deadline))
        for task in list(pending):
            kind, which, ready, deadline = task
            if ready == k:
                pending.remove(task)
                due.setdefault(deadline, []).append(compute(kind, which, [landed[k]]))
    for kind, which, _, _ in pending:
        compute(kind, which, [])
    return out.reshape(half * width, width)


def solution(mesh):
    placed = (P(("grp", "tok"), "head"), P(("grp", "tok"), None), P(("grp", "tok"), None), P())
    return jax.shard_map(
        functools.partial(local, mesh.shape["head"]),
        mesh=mesh,
        in_specs=placed,
        out_specs=P(("grp", "tok"), "head"),
        check_vma=False,
    )
```
